32 devices in a mesh: dom: 8 (over z, y), band: 4 (over x, core).
Axes of the slice: x: 2, y: 2, z: 4, core: 2. Of those that a mesh axis runs over, the one named last changes fastest.
Arguments:
- orbitals: float32 [8, 128, 24, 576], P('dom', 'band'), may hold values from -6 to 6
- potential: float32 [8, 24, 576], P('dom'), may hold values from 0 to 3
- density_in: float32 [8, 24, 576], P('dom', 'band'), may hold values from 0.3 to 3
- occupation: float32 [128], replicated, may hold values from 0.5 to 2
- position: int32 [8], replicated, may hold values from 0 to 7, each once
- mixing: int32 [2], replicated, may hold values from 1 to 8
- correlation_weight: int32 [6], replicated, may hold values from 1 to 15
Outputs:
- orbitals_out: float32 [8, 128, 24, 576], P('dom', None, 'band')
- density: float32 [8, 24, 576], P('dom', 'band')
- hartree: float32 [8, 8, 8, 6], P('dom', 'band')
The draws below stay inside these ranges and needn't reach their ends.
Inputs may be any that keep to these rules, and one draw needn't show every extreme that they name: position is a permutation: every place along the chain holds exactly one domain.
All inputs are finite; a program needn't handle non-finite values.
Results may differ from the reference program's by a relative error of at most 0.0001.
Values sent between devices are 32-bit elements; how exact they have to be, the bound alone decides.
A program may use at most 64 MiB of HBM per device.

```python
import math
import jax
import jax.numpy as jnp
from jax import lax

NB = 128
G = 24
BUFFER = 6
COARSEN = 3
DEGREE = 2
NS_STEPS = 2
DOMAINS = 8
CG = 8
CZ = 6
NZC = 48
N_DOM = 8


def with_ends(result, own_key, least, largest):
    shape = result.shape
    place = [jax.random.randint(jax.random.fold_in(own_key, axis), (), 0, shape[axis]) for axis in range(len(shape))]
    result = result.at[tuple(place)].set(least)
    longest = shape.index(max(shape))
    place[longest] = (place[longest] + 1) % shape[longest]
    return result.at[tuple(place)].set(largest)


def levels(key, shape, cuts, low, largest):
    level, own = 1.0, jax.random.fold_in(key, 6)
    for dim, shards_of in cuts:
        draws = jnp.exp(jax.random.uniform(jax.random.fold_in(own, dim), (shards_of,), jnp.float32, low / len(cuts), largest / len(cuts)))
        level = level * jnp.repeat(draws, shape[dim] // shards_of).reshape([-1 if axis == dim else 1 for axis in range(len(shape))])
    return level


def bell_draw(own_key, dims, deviation, most, cuts=(), kind=jnp.bfloat16):
    values = deviation * jax.random.normal(own_key, dims, jnp.float32)
    if cuts:
        values = values * levels(own_key, dims, cuts, -0.22, 0.18)
    return jnp.clip(values, -most, most).astype(kind)


def setup_inputs(seed: int = 0) -> dict:
    keys = jax.random.split(jax.random.key(seed), 8)
    return {
        "orbitals": bell_draw(keys[0], (DOMAINS, NB, G, G * G), 1.0, 6.0, ((0, 8), (1, 4)), jnp.float32),
        "potential": jnp.clip(3.0 * jax.random.uniform(keys[1], (DOMAINS, G, G * G), jnp.float32) ** levels(keys[1], (DOMAINS, G, G * G), ((0, 8),), -0.2, 0.2), 0.0, 3.0),
        "density_in": jnp.clip(jnp.exp(math.log(3.0) - 2.3025851 * jax.random.uniform(keys[2], (DOMAINS, G, G * G), jnp.float32) ** levels(keys[2], (DOMAINS, G, G * G), ((0, 8), (1, 4)), -0.2, 0.2)), 0.3, 3.0),
        "occupation": jnp.clip(jax.random.uniform(keys[3], (NB,), jnp.float32, 0.5, 2.0), 0.5, 2.0),
        "position": jax.random.permutation(keys[4], DOMAINS).astype(jnp.int32),
        "mixing": jax.random.randint(keys[5], (2,), 1, 9).astype(jnp.int32),
        "correlation_weight": with_ends(jax.random.randint(keys[6], (BUFFER,), 1, 16), jax.random.fold_in(keys[6], 1), 1, 15).astype(jnp.int32),
    }


HIGHEST = lax.Precision.HIGHEST
filter_low = 1.0
filter_high = 9.5
blend_total = 16.0

def sine_entries(row_values, col_values, extent):
    products = (row_values[:, None] + 1.0) * (col_values[None, :] + 1.0)
    return jnp.sqrt(2.0 / (extent + 1.0)) * jnp.sin(jnp.pi * products / (extent + 1.0))

def sine_table(extent):
    indices = jnp.arange(extent, dtype=jnp.float32)
    return sine_entries(indices, indices, extent)

def cosine_table(extent):
    indices = jnp.arange(extent, dtype=jnp.float32)
    entries = jnp.sqrt(2.0 / extent) * jnp.cos(jnp.pi * indices[:, None] * (indices[None, :] + 0.5) / extent)
    return entries * jnp.where(indices == 0.0, jnp.sqrt(0.5), 1.0)[:, None]

def lap_eigen(indices, extent, shift_by):
    half_angle = 0.5 * jnp.pi * (indices + shift_by) / (extent + shift_by)
    return 4.0 * jnp.sin(half_angle) ** 2

def kinetic_table(extent):
    indices = jnp.arange(extent, dtype=jnp.float32)
    single = 0.5 * lap_eigen(indices, extent, 1.0)
    plane_values = single[:, None] + single[None, :]
    return single[:, None] + plane_values.reshape(1, extent * extent)

def transform(values, sine_matrix, plane_matrix):
    values = jnp.einsum('bxc,xk->bkc', values, sine_matrix, precision=HIGHEST)
    return jnp.einsum('bxc,cd->bxd', values, plane_matrix, precision=HIGHEST)

def apply_hamil(values, potential_grid, sine_matrix, plane_matrix, kinetic):
    spectral = kinetic * transform(values, sine_matrix, plane_matrix)
    return transform(spectral, sine_matrix, plane_matrix) + potential_grid * values

def chebyshev(orbital_block, potential_grid, sine_matrix, plane_matrix, kinetic):
    center = 0.5 * (filter_high + filter_low)
    half_width = 0.5 * (filter_high - filter_low)

    def shifted(values):
        return (apply_hamil(values, potential_grid, sine_matrix, plane_matrix, kinetic) - center * values) / half_width
    before = orbital_block
    current = shifted(orbital_block)
    for repeat in range(DEGREE - 1):
        newest = 2.0 * shifted(current) - before
        before, current = (current, newest)
    return current

def reference(orbitals, potential, density_in, occupation, position, mixing, correlation_weight):
    sine_matrix = sine_table(G)
    plane_matrix = jnp.kron(sine_matrix, sine_matrix)
    kinetic = kinetic_table(G)
    points = float(G * G * G)

    def one_domain(inputs):
        orbital_block, potential_grid = inputs
        filtered = chebyshev(orbital_block, potential_grid, sine_matrix, plane_matrix, kinetic)
        flat_orbitals = filtered.reshape(NB, G * G * G)
        correlation_raw = jnp.dot(flat_orbitals, flat_orbitals.T, precision=HIGHEST)
        norm_fro = jnp.sqrt(jnp.sum(correlation_raw * correlation_raw))
        current = flat_orbitals * jnp.sqrt(points / norm_fro)
        correlation = correlation_raw / norm_fro
        for iteration in range(NS_STEPS):
            if iteration > 0:
                correlation = jnp.dot(current, current.T, precision=HIGHEST) / points
            current = 1.5 * current - 0.5 * jnp.dot(correlation, current, precision=HIGHEST)
        density_row = jnp.dot(occupation, current * current, precision=HIGHEST) / NB
        return (current.reshape(NB, G, G * G), density_row.reshape(G, G, G))
    orbitals_out, fresh_cube = lax.map(one_domain, (orbitals, potential))
    indices = jnp.arange(N_DOM, dtype=jnp.int32)
    left_of = lax.optimization_barrier(jnp.sum(jnp.where(position[None, :] == position[:, None] - 1, indices[None, :], 0), axis=1)).astype(jnp.int32)
    right_of = lax.optimization_barrier(jnp.sum(jnp.where(position[None, :] == position[:, None] + 1, indices[None, :], 0), axis=1)).astype(jnp.int32)
    has_left = (position > 0)[:, None, None, None]
    has_right = (position < N_DOM - 1)[:, None, None, None]
    weight_left = correlation_weight.astype(jnp.float32)
    own_low = fresh_cube[..., :BUFFER]
    own_high = fresh_cube[..., G - BUFFER:]
    left_high = jnp.take(fresh_cube, left_of, axis=0)[..., G - BUFFER:]
    right_low = jnp.take(fresh_cube, right_of, axis=0)[..., :BUFFER]
    blend_low = jnp.where(has_left, (weight_left * left_high + (blend_total - weight_left) * own_low) / blend_total, own_low)
    blend_high = jnp.where(has_right, (weight_left * own_high + (blend_total - weight_left) * right_low) / blend_total, own_high)
    blended = jnp.concatenate([blend_low, fresh_cube[..., BUFFER:G - BUFFER], blend_high], 3)
    mix_weights = mixing.astype(jnp.float32)
    inflow = density_in.reshape(N_DOM, G, G, G)
    mixed_density = (mix_weights[0] * blended + mix_weights[1] * inflow) / (mix_weights[0] + mix_weights[1])
    density = mixed_density.reshape(N_DOM, G, G * G)
    core_cells = mixed_density[..., :G - BUFFER].reshape(N_DOM, CG, COARSEN, CG, COARSEN, CZ, COARSEN)
    coarse = lax.optimization_barrier(jnp.sum(core_cells, axis=(2, 4, 6))) / float(COARSEN ** 3)
    dom_at = lax.optimization_barrier(jnp.sum(jnp.where(position[None, :] == indices[:, None], indices[None, :], 0), axis=1)).astype(jnp.int32)
    chain_grid = jnp.take(coarse, dom_at, axis=0)
    chain_grid = jnp.transpose(chain_grid, (1, 2, 0, 3)).reshape(CG * CG, NZC)
    sine_chain = sine_table(NZC)
    cross_table = jnp.kron(cosine_table(CG), cosine_table(CG))
    level_x = lap_eigen(jnp.arange(CG, dtype=jnp.float32), CG, 0.0)
    level_xy = (level_x[:, None] + level_x[None, :]).reshape(CG * CG)
    level_z = lap_eigen(jnp.arange(NZC, dtype=jnp.float32), NZC, 1.0)
    spectrum = jnp.dot(cross_table, jnp.dot(chain_grid, sine_chain, precision=HIGHEST), precision=HIGHEST)
    spectrum = spectrum / (level_xy[:, None] + level_z[None, :])
    field_grid = jnp.dot(cross_table.T, jnp.dot(spectrum, sine_chain, precision=HIGHEST), precision=HIGHEST)
    field_grid = field_grid * (8.0 / float(NZC * NZC))
    field_grid = field_grid.reshape(CG, CG, N_DOM, CZ)
    hartree = jnp.transpose(jnp.take(field_grid, position, axis=2), (2, 0, 1, 3))
    return (orbitals_out, density, hartree)
```

```python
import functools

import jax
import jax.numpy as jnp
import ml_dtypes
import numpy as np
from jax import lax
from jax.experimental import pallas as pl
from jax.experimental.pallas import tpu as pltpu
from jax.sharding import PartitionSpec as P

BUFFER = 6
COARSEN = 3
CG = 8
CZ = 6
ROWS = 8
CENTER = 5.25
HALF_WIDTH = 4.25
BLEND_TOTAL = 16.0
HIGHEST = lax.Precision.HIGHEST
MESH = pl.DeviceIdType.MESH
F32, BF16 = jnp.float32, jnp.bfloat16


def split_np(table):
    high = table.astype(ml_dtypes.bfloat16)
    return high, (table - high.astype(np.float64)).astype(ml_dtypes.bfloat16)


def tables(grid, dom_count, band_count):
    line = np.eye(grid, k=1) + np.eye(grid, k=-1)
    adjacency = np.kron(line, np.eye(grid)) + np.kron(np.eye(grid), line)
    along_y = np.zeros((grid, CG))
    along_y[np.arange(grid), np.arange(grid) // COARSEN] = 1.0
    along_z = np.zeros((grid, CZ))
    core = np.arange(CZ * COARSEN)
    along_z[core, core // COARSEN] = 1.0
    coarsen = np.kron(along_y, along_z)
    order = np.arange(CG)
    cosine = np.sqrt(2.0 / CG) * np.cos(np.pi * order[:, None] * (order[None, :] + 0.5) / CG)
    cosine[0] *= np.sqrt(0.5)
    chain = dom_count * CZ
    place = np.arange(chain)
    sine = np.sqrt(2.0 / (chain + 1)) * np.sin(
        np.pi * (place[:, None] + 1.0) * (place[None, :] + 1.0) / (chain + 1)
    )
    spectral = np.einsum("ky,pzq->pyzkq", cosine, sine.reshape(dom_count, CZ, chain)).reshape(
        dom_count * CG * CZ, CG * chain
    )
    planes = grid // band_count
    coarse_x = planes // COARSEN
    forward = np.zeros((CG, band_count, ROWS))
    backward = np.zeros((band_count, ROWS, CG))
    for band in range(band_count):
        for plane in range(planes):
            forward[:, band, plane] = cosine[:, band * coarse_x + plane // COARSEN] / COARSEN**3
        for cell in range(coarse_x):
            backward[band, cell] = cosine[:, band * coarse_x + cell]
    side = 4.0 * np.sin(0.5 * np.pi * order / CG) ** 2
    depth = 4.0 * np.sin(0.5 * np.pi * (place + 1.0) / (chain + 1.0)) ** 2
    eigen = side[:, None, None] + side[None, :, None] + depth[None, None, :]
    inverse = (8.0 / chain**2 / eigen).reshape(CG, CG * chain)
    spectral_high, spectral_low = split_np(spectral)
    return (
        adjacency.astype(ml_dtypes.bfloat16),
        coarsen.astype(ml_dtypes.bfloat16),
        spectral_high,
        spectral_low,
        forward.reshape(CG, band_count * ROWS).astype(np.float32),
        backward.reshape(band_count * ROWS, CG).astype(np.float32),
        inverse.astype(np.float32),
    )


def split(values):
    high = values.astype(BF16)
    return high, (values - high.astype(F32)).astype(BF16)


def dot(a, b, precision=None):
    return jnp.dot(a, b, preferred_element_type=F32, precision=precision)


def dot_nt(a, b):
    return lax.dot_general(a, b, (((1,), (1,)), ((), ())), preferred_element_type=F32)


def kernel(
    sizes,
    orb_ref, pot_ref, din_ref, occ_ref, pos_ref, mix_ref, cw_ref,
    adj_ref, coarsen_ref, sph_ref, spl_ref, fwd_ref, bwd_ref, inv_ref,
    out_ref, den_ref, har_ref,
    diag, filt, full, parts, raw_src, raw_in, din_src, din_all, fresh_src, fresh_all,
    spec_src, spec_all, own_h, own_l,
    a2a_send, a2a_recv, raw_send, raw_recv, din_send, din_recv, fr_send, fr_recv, sp_send, sp_recv,
):
    grid, cells, nb, local, planes, n_dom, n_band = sizes
    dom, band = lax.axis_index("dom"), lax.axis_index("band")
    shifts = [r for r in range(1, n_band)]
    shifts.sort(key=lambda r: r % 2)
    chunks = local // 8

    barrier = pltpu.get_barrier_semaphore()
    for r in range(1, n_band):
        pl.semaphore_signal(barrier, inc=1, device_id={"band": lax.rem(band + r, n_band)}, device_id_type=MESH)
    for r in range(1, n_dom):
        pl.semaphore_signal(barrier, inc=1, device_id={"dom": lax.rem(dom + r, n_dom)}, device_id_type=MESH)

    for k in range(grid):
        row = (3.0 - CENTER + pot_ref[pl.ds(k, 1), :]) * (1.0 / HALF_WIDTH)
        diag[k] = jnp.broadcast_to(row, (8, cells))
    if planes < ROWS:
        din_src[...] = jnp.zeros_like(din_src)
        fresh_src[...] = jnp.zeros_like(fresh_src)
    din_src[pl.ds(0, planes), :] = din_ref[...]

    def neighbours(values):
        flat = values.reshape(grid * 8, cells)
        high, low = split(flat)
        both = dot(jnp.concatenate([high, low], 0), adj_ref[...])
        inside = (both[: grid * 8] + both[grid * 8 :]).reshape(grid, 8, cells)
        edge = jnp.zeros((1, 8, cells), F32)
        return (
            inside
            + jnp.concatenate([edge, values[:-1]], 0)
            + jnp.concatenate([values[1:], edge], 0)
        )

    def a2a_copy(r, c, start):
        peer = lax.rem(band + r, n_band)
        return pltpu.make_async_remote_copy(
            src_ref=filt.at[pl.ds(peer * planes, planes), pl.ds(start, 8), :],
            dst_ref=full.at[:, pl.ds(pl.multiple_of(band * local + start, 8), 8), :],
            send_sem=a2a_send.at[r - 1, c],
            recv_sem=a2a_recv.at[r - 1, c],
            device_id={"band": peer},
            device_id_type=MESH,
        )

    def filter_chunk(c):
        start = pl.multiple_of(c * 8, 8)
        first = orb_ref[:, pl.ds(start, 8), :]
        once = diag[...] * first - (0.5 / HALF_WIDTH) * neighbours(first)
        twice = 2.0 * (diag[...] * once - (0.5 / HALF_WIDTH) * neighbours(once)) - first
        filt[:, pl.ds(start, 8), :] = twice

    def send_chunk(c):
        start = pl.multiple_of(c * 8, 8)
        for r in shifts:
            a2a_copy(r, c, start).start()
        full[:, pl.ds(pl.multiple_of(band * local + start, 8), 8), :] = filt[
            pl.ds(band * planes, planes), pl.ds(start, 8), :
        ]

    filter_chunk(0)
    pl.semaphore_wait(barrier, n_band + n_dom - 2)
    send_chunk(0)

    def step(c, carry):
        filter_chunk(c)
        send_chunk(c)
        return carry

    lax.fori_loop(1, chunks, step, 0)

    def dom_copy(src, dst, send, recv, r):
        return pltpu.make_async_remote_copy(
            src_ref=src, dst_ref=dst.at[dom], send_sem=send.at[r - 1], recv_sem=recv.at[r - 1],
            device_id={"dom": lax.rem(dom + r, n_dom)}, device_id_type=MESH,
        )

    def band_copy(src, dst, send, recv, r):
        return pltpu.make_async_remote_copy(
            src_ref=src, dst_ref=dst.at[band], send_sem=send.at[r - 1], recv_sem=recv.at[r - 1],
            device_id={"band": lax.rem(band + r, n_band)}, device_id_type=MESH,
        )

    din_copies = [dom_copy(din_src, din_all, din_send, din_recv, r) for r in range(1, n_dom)]
    for copy in din_copies:
        copy.start()
    din_all[dom] = din_src[...]

    places = [pos_ref[d] for d in range(n_dom)]
    own_place = jnp.int32(0)
    for d in range(n_dom):
        own_place = own_place + jnp.where(dom == d, places[d], 0)
    block = CG * CZ
    total_h = jnp.zeros(own_h.shape, F32)
    total_l = jnp.zeros(own_l.shape, F32)
    for p in range(n_dom):
        pick = jnp.where(own_place == p, 1.0, 0.0).astype(F32)
        total_h = total_h + pick * sph_ref[pl.ds(p * block, block), :].astype(F32)
        total_l = total_l + pick * spl_ref[pl.ds(p * block, block), :].astype(F32)
    own_h[...] = total_h.astype(BF16)
    own_l[...] = total_l.astype(BF16)
    z = lax.rem(lax.broadcasted_iota(jnp.int32, (1, cells), 1), grid)
    weight = jnp.zeros((1, cells), F32)
    for j in range(BUFFER):
        value = cw_ref[j].astype(F32)
        weight = weight + jnp.where((z == j) | (z == grid - BUFFER + j), value, 0.0)
    row_id = lax.broadcasted_iota(jnp.int32, (nb, nb), 0)
    col_id = lax.broadcasted_iota(jnp.int32, (nb, nb), 1)
    eye = jnp.where(row_id == col_id, 1.0, 0.0).astype(F32)
    occupation = jnp.sum(eye * occ_ref[...], axis=1, keepdims=True)

    def wait_chunk(c, carry):
        start = pl.multiple_of(c * 8, 8)
        for r in shifts:
            a2a_copy(r, c, start).wait()
        return carry

    lax.fori_loop(0, chunks, wait_chunk, 0)

    product = jnp.zeros((nb, 2 * nb), F32)
    for k in range(planes):
        high, low = split(full[k])
        parts[k, pl.ds(0, nb), :] = high
        parts[k, pl.ds(nb, nb), :] = low
        product = product + dot_nt(high, parts[k])
    cross = product[:, nb:]
    raw_src[...] = product[:, :nb] + cross + cross.T
    raw_copies = [band_copy(raw_src, raw_in, raw_send, raw_recv, r) for r in shifts]
    for copy in raw_copies:
        copy.start()
    raw_in[band] = raw_src[...]
    for copy in raw_copies:
        copy.wait()
    raw = raw_in[0]
    for b in range(1, n_band):
        raw = raw + raw_in[b]
    norm = jnp.sqrt(jnp.sum(raw * raw, keepdims=True))
    scaling = jnp.sqrt(float(grid**3) / norm)
    gram = raw / norm
    linear = 1.5 * eye - 0.5 * gram
    cubic = dot(dot(linear, gram, HIGHEST), dot(linear, linear, HIGHEST), HIGHEST)
    poly = scaling * (1.5 * linear - 0.5 * cubic)
    poly_high, poly_low = split(poly)
    poly_twice = jnp.concatenate([poly_high, poly_high], 1)
    for k in range(planes):
        result = dot(poly_twice, parts[k]) + dot(poly_low, parts[k, pl.ds(0, nb), :])
        out_ref[k] = result
        fresh_src[pl.ds(k, 1), :] = jnp.sum(occupation * (result * result), axis=0, keepdims=True) * (1.0 / nb)

    fresh_copies = [dom_copy(fresh_src, fresh_all, fr_send, fr_recv, r) for r in range(1, n_dom)]
    for copy in fresh_copies:
        copy.start()
    fresh_all[dom] = fresh_src[...]
    for copy in din_copies:
        copy.wait()

    def ordered(ref):
        rows = []
        for p in range(n_dom):
            total = jnp.zeros((ROWS, cells), F32)
            for d in range(n_dom):
                total = total + jnp.where(places[d] == p, 1.0, 0.0).astype(F32) * ref[d]
            rows.append(total)
        return rows

    inflow = ordered(din_all)
    for copy in fresh_copies:
        copy.wait()
    fresh = ordered(fresh_all)

    gap = grid - BUFFER
    mix_new = jnp.full((1, cells), mix_ref[0].astype(F32))
    mix_old = jnp.full((1, cells), mix_ref[1].astype(F32))
    mixed = []
    own_density = jnp.zeros((ROWS, cells), F32)
    for p in range(n_dom):
        own = fresh[p]
        blended = own
        if p > 0:
            left = jnp.concatenate([fresh[p - 1][:, gap:], fresh[p - 1][:, :gap]], 1)
            low = (weight * left + (BLEND_TOTAL - weight) * own) / BLEND_TOTAL
            blended = jnp.where(z < BUFFER, low, blended)
        if p < n_dom - 1:
            right = jnp.concatenate([fresh[p + 1][:, cells - gap :], fresh[p + 1][:, : cells - gap]], 1)
            high = (weight * own + (BLEND_TOTAL - weight) * right) / BLEND_TOTAL
            blended = jnp.where(z >= gap, high, blended)
        value = (mix_new * blended + mix_old * inflow[p]) / (mix_new + mix_old)
        mixed.append(value)
        own_density = own_density + jnp.where(own_place == p, 1.0, 0.0).astype(F32) * value
    den_ref[...] = own_density[:planes]

    stacked = jnp.concatenate(mixed, 0)
    height = n_dom * ROWS
    high, low = split(stacked)
    both = dot(jnp.concatenate([high, low], 0), coarsen_ref[...])
    coarse = both[:height] + both[height:]
    wide = jnp.concatenate([coarse[p * ROWS : (p + 1) * ROWS] for p in range(n_dom)], 1)
    high, low = split(wide)
    spec_src[...] = dot(high, sph_ref[...]) + dot(low, sph_ref[...]) + dot(high, spl_ref[...])
    spec_copies = [band_copy(spec_src, spec_all, sp_send, sp_recv, r) for r in shifts]
    for copy in spec_copies:
        copy.start()
    spec_all[band] = spec_src[...]
    for copy in spec_copies:
        copy.wait()
    gathered = spec_all[...].reshape(n_band * ROWS, spec_src.shape[1])
    spectrum = dot(fwd_ref[...], gathered, HIGHEST) * inv_ref[...]
    mine = dot(bwd_ref[pl.ds(pl.multiple_of(band * ROWS, ROWS), ROWS), :], spectrum, HIGHEST)
    high, low = split(mine)
    field = dot_nt(high, own_h[...]) + dot_nt(low, own_h[...]) + dot_nt(high, own_l[...])
    har_ref[...] = field[: har_ref.shape[0]]


def body(orbitals, potential, density_in, occupation, position, mixing, correlation_weight):
    nb = occupation.shape[0]
    n_dom, n_band = lax.axis_size("dom"), lax.axis_size("band")
    _, local, grid, cells = orbitals.shape
    planes = density_in.shape[1]
    coarse_x = planes // COARSEN
    chain = CG * CZ * n_dom
    sizes = (grid, cells, nb, local, planes, n_dom, n_band)
    vmem = pl.BlockSpec(memory_space=pltpu.VMEM)
    smem = pl.BlockSpec(memory_space=pltpu.SMEM)
    consts = [jnp.asarray(t) for t in tables(grid, n_dom, n_band)]
    dma = pltpu.SemaphoreType.DMA
    chunks = local // 8
    out, density, hartree = pl.pallas_call(
        functools.partial(kernel, sizes),
        out_shape=(
            jax.ShapeDtypeStruct((planes, nb, cells), F32),
            jax.ShapeDtypeStruct((planes, cells), F32),
            jax.ShapeDtypeStruct((coarse_x, CG * CZ), F32),
        ),
        in_specs=[vmem] * 4 + [smem] * 3 + [vmem] * 7,
        out_specs=(vmem, vmem, vmem),
        scratch_shapes=[
            pltpu.VMEM((grid, 8, cells), F32),
            pltpu.VMEM((grid, local, cells), F32),
            pltpu.VMEM((planes, nb, cells), F32),
            pltpu.VMEM((planes, 2 * nb, cells), BF16),
            pltpu.VMEM((nb, nb), F32),
            pltpu.VMEM((n_band, nb, nb), F32),
            pltpu.VMEM((ROWS, cells), F32),
            pltpu.VMEM((n_dom, ROWS, cells), F32),
            pltpu.VMEM((ROWS, cells), F32),
            pltpu.VMEM((n_dom, ROWS, cells), F32),
            pltpu.VMEM((ROWS, chain), F32),
            pltpu.VMEM((n_band, ROWS, chain), F32),
            pltpu.VMEM((CG * CZ, chain), BF16),
            pltpu.VMEM((CG * CZ, chain), BF16),
            dma((n_band - 1, chunks)), dma((n_band - 1, chunks)),
            dma((n_band - 1,)), dma((n_band - 1,)),
            dma((n_dom - 1,)), dma((n_dom - 1,)),
            dma((n_dom - 1,)), dma((n_dom - 1,)),
            dma((n_band - 1,)), dma((n_band - 1,)),
        ],
        compiler_params=pltpu.CompilerParams(
            collective_id=0, has_side_effects=True, vmem_limit_bytes=56 * 1024 * 1024
        ),
    )(
        jnp.swapaxes(orbitals[0], 0, 1), potential[0], density_in[0], occupation.reshape(1, nb),
        position, mixing, correlation_weight, *consts,
    )
    return (
        jnp.swapaxes(out, 0, 1)[None],
        density[None],
        hartree.reshape(1, coarse_x, CG, CZ),
    )


def solution(mesh):
    return jax.shard_map(
        body,
        mesh=mesh,
        in_specs=(
            P("dom", "band", None, None),
            P("dom", None, None),
            P("dom", "band", None),
            P(),
            P(),
            P(),
            P(),
        ),
        out_specs=(
            P("dom", None, "band", None),
            P("dom", "band", None),
            P("dom", "band", None, None),
        ),
        check_vma=False,
    )
```

```python
import functools

import jax
import jax.numpy as jnp
import ml_dtypes
import numpy as np
from jax import lax
from jax.experimental import pallas as pl
from jax.experimental.pallas import tpu as pltpu
from jax.sharding import PartitionSpec as P

BUFFER = 6
COARSEN = 3
CG = 8
CZ = 6
ROWS = 8
CENTER = 5.25
HALF_WIDTH = 4.25
BLEND_TOTAL = 16.0
HIGHEST = lax.Precision.HIGHEST
MESH = pl.DeviceIdType.MESH
F32, BF16 = jnp.float32, jnp.bfloat16


def split_np(table):
    high = table.astype(ml_dtypes.bfloat16)
    return high, (table - high.astype(np.float64)).astype(ml_dtypes.bfloat16)


def tables(grid, dom_count, band_count):
    along_y = np.zeros((grid, CG))
    along_y[np.arange(grid), np.arange(grid) // COARSEN] = 1.0
    along_z = np.zeros((grid, CZ))
    core = np.arange(CZ * COARSEN)
    along_z[core, core // COARSEN] = 1.0
    coarsen = np.einsum("yY,zZ->yzZY", along_y, along_z).reshape(grid * grid, CZ * CG)
    order = np.arange(CG)
    cosine = np.sqrt(2.0 / CG) * np.cos(np.pi * order[:, None] * (order[None, :] + 0.5) / CG)
    cosine[0] *= np.sqrt(0.5)
    chain = dom_count * CZ
    place = np.arange(chain)
    sine = np.sqrt(2.0 / (chain + 1)) * np.sin(
        np.pi * (place[:, None] + 1.0) * (place[None, :] + 1.0) / (chain + 1)
    )
    spectral = np.einsum("ky,pzq->pzykq", cosine, sine.reshape(dom_count, CZ, chain)).reshape(
        dom_count * CG * CZ, CG * chain
    )
    planes = grid // band_count
    coarse_x = planes // COARSEN
    forward = np.zeros((CG, band_count, ROWS))
    backward = np.zeros((band_count, ROWS, CG))
    for band in range(band_count):
        for plane in range(planes):
            forward[:, band, plane] = cosine[:, band * coarse_x + plane // COARSEN] / COARSEN**3
        for cell in range(coarse_x):
            backward[band, cell] = cosine[:, band * coarse_x + cell]
    side = 4.0 * np.sin(0.5 * np.pi * order / CG) ** 2
    depth = 4.0 * np.sin(0.5 * np.pi * (place + 1.0) / (chain + 1.0)) ** 2
    eigen = side[:, None, None] + side[None, :, None] + depth[None, None, :]
    inverse = (8.0 / chain**2 / eigen).reshape(CG, CG * chain)
    spectral_high, spectral_low = split_np(spectral)
    return (
        coarsen.astype(ml_dtypes.bfloat16),
        spectral_high,
        spectral_low,
        forward.reshape(CG, band_count * ROWS).astype(np.float32),
        backward.reshape(band_count * ROWS, CG).astype(np.float32),
        inverse.astype(np.float32),
    )


def split(values):
    high = values.astype(BF16)
    return high, (values - high.astype(F32)).astype(BF16)


def dot(a, b, precision=None):
    return jnp.dot(a, b, preferred_element_type=F32, precision=precision)


def dot_nt(a, b):
    return lax.dot_general(a, b, (((1,), (1,)), ((), ())), preferred_element_type=F32)


def kernel(
    sizes,
    orb_ref, pot_ref, din_ref, occ_ref, pos_ref, mix_ref, cw_ref,
    coarsen_ref, sph_ref, spl_ref, fwd_ref, bwd_ref, inv_ref,
    out_ref, den_ref, har_ref,
    diag, before, once, filt, full, result, parts, raw_src, raw_in, din_src, din_all, fresh_src, fresh_all,
    spec_src, spec_all, own_h, own_l,
    a2a_send, a2a_recv, raw_send, raw_recv, din_send, din_recv, fr_send, fr_recv, sp_send, sp_recv,
):
    grid, cells, nb, local, planes, pack, n_dom, n_band = sizes
    groups = planes // pack
    dom, band = lax.axis_index("dom"), lax.axis_index("band")
    shifts = [r for r in range(1, n_band)]
    shifts.sort(key=lambda r: r % 2)
    chunks = local // 8

    barrier = pltpu.get_barrier_semaphore()
    for r in range(1, n_band):
        pl.semaphore_signal(barrier, inc=1, device_id={"band": lax.rem(band + r, n_band)}, device_id_type=MESH)
    for r in range(1, n_dom):
        pl.semaphore_signal(barrier, inc=1, device_id={"dom": lax.rem(dom + r, n_dom)}, device_id_type=MESH)

    wide_cells = diag.shape[2]
    lane = lax.broadcasted_iota(jnp.int32, (8, wide_cells), 1)
    depth = lax.rem(lane, grid)
    inside = jnp.where(lane < cells, 1.0, 0.0).astype(F32)
    above = jnp.where((lane < cells) & (depth > 0), 1.0, 0.0).astype(F32)
    below = jnp.where((lane < cells) & (depth < grid - 1), 1.0, 0.0).astype(F32)
    for k in range(grid):
        row = (3.0 - CENTER + pot_ref[pl.ds(k, 1), :]) * (1.0 / HALF_WIDTH)
        diag[k, :, pl.ds(0, cells)] = jnp.broadcast_to(row, (8, cells))
        for ref in (diag, before):
            ref[k, :, pl.ds(cells, wide_cells - cells)] = jnp.zeros((8, wide_cells - cells), F32)
    if planes < ROWS:
        din_src[...] = jnp.zeros_like(din_src)
        fresh_src[...] = jnp.zeros_like(fresh_src)
    din_src[pl.ds(0, planes), :] = din_ref[:, 0, :]

    def shifted(ref, k):
        here = ref[k]
        total = pltpu.roll(here, grid, 1) + pltpu.roll(here, wide_cells - grid, 1)
        total = total + above * pltpu.roll(here, 1, 1) + below * pltpu.roll(here, wide_cells - 1, 1)
        if k > 0:
            total = total + ref[k - 1]
        if k < grid - 1:
            total = total + ref[k + 1]
        return diag[k] * here - (0.5 / HALF_WIDTH) * total

    def a2a_copy(r, c, start):
        peer = lax.rem(band + r, n_band)
        return pltpu.make_async_remote_copy(
            src_ref=filt.at[pl.ds(peer * groups, groups), pl.ds(start, 8), :],
            dst_ref=full.at[:, pl.ds(pl.multiple_of(band * local + start, 8), 8), :],
            send_sem=a2a_send.at[r - 1, c],
            recv_sem=a2a_recv.at[r - 1, c],
            device_id={"band": peer},
            device_id_type=MESH,
        )

    def filter_chunk(c):
        start = pl.multiple_of(c * 8, 8)
        before[:, :, pl.ds(0, cells)] = jnp.swapaxes(orb_ref[pl.ds(start, 8)], 0, 1)
        for k in range(grid):
            once[k] = inside * shifted(before, k)
        for j in range(grid // pack):
            pieces = [
                (2.0 * shifted(once, k) - before[k])[:, :cells] for k in range(j * pack, (j + 1) * pack)
            ]
            filt[j, pl.ds(start, 8), :] = pieces[0] if pack == 1 else jnp.concatenate(pieces, 1)

    def send_chunk(c):
        start = pl.multiple_of(c * 8, 8)
        for r in shifts:
            a2a_copy(r, c, start).start()
        full[:, pl.ds(pl.multiple_of(band * local + start, 8), 8), :] = filt[
            pl.ds(band * groups, groups), pl.ds(start, 8), :
        ]

    filter_chunk(0)
    pl.semaphore_wait(barrier, n_band + n_dom - 2)
    send_chunk(0)

    def step(c, carry):
        filter_chunk(c)
        send_chunk(c)
        return carry

    lax.fori_loop(1, chunks, step, 0)

    def dom_copy(src, dst, send, recv, r):
        return pltpu.make_async_remote_copy(
            src_ref=src, dst_ref=dst.at[dom], send_sem=send.at[r - 1], recv_sem=recv.at[r - 1],
            device_id={"dom": lax.rem(dom + r, n_dom)}, device_id_type=MESH,
        )

    def band_copy(src, dst, send, recv, r):
        return pltpu.make_async_remote_copy(
            src_ref=src, dst_ref=dst.at[band], send_sem=send.at[r - 1], recv_sem=recv.at[r - 1],
            device_id={"band": lax.rem(band + r, n_band)}, device_id_type=MESH,
        )

    din_copies = [dom_copy(din_src, din_all, din_send, din_recv, r) for r in range(1, n_dom)]
    for copy in din_copies:
        copy.start()
    din_all[dom] = din_src[...]

    places = [pos_ref[d] for d in range(n_dom)]
    own_place = jnp.int32(0)
    for d in range(n_dom):
        own_place = own_place + jnp.where(dom == d, places[d], 0)
    block = CG * CZ
    total_h = jnp.zeros(own_h.shape, F32)
    total_l = jnp.zeros(own_l.shape, F32)
    for p in range(n_dom):
        pick = jnp.where(own_place == p, 1.0, 0.0).astype(F32)
        total_h = total_h + pick * sph_ref[pl.ds(p * block, block), :].astype(F32)
        total_l = total_l + pick * spl_ref[pl.ds(p * block, block), :].astype(F32)
    own_h[...] = total_h.astype(BF16)
    own_l[...] = total_l.astype(BF16)
    z = lax.rem(lax.broadcasted_iota(jnp.int32, (1, cells), 1), grid)
    weight = jnp.zeros((1, cells), F32)
    for j in range(BUFFER):
        value = cw_ref[j].astype(F32)
        weight = weight + jnp.where((z == j) | (z == grid - BUFFER + j), value, 0.0)
    row_id = lax.broadcasted_iota(jnp.int32, (nb, nb), 0)
    col_id = lax.broadcasted_iota(jnp.int32, (nb, nb), 1)
    eye = jnp.where(row_id == col_id, 1.0, 0.0).astype(F32)
    occupation = jnp.sum(eye * occ_ref[...], axis=1, keepdims=True)

    def wait_chunk(c, carry):
        start = pl.multiple_of(c * 8, 8)
        for r in shifts:
            a2a_copy(r, c, start).wait()
        return carry

    lax.fori_loop(0, chunks, wait_chunk, 0)

    product = jnp.zeros((nb, 2 * nb), F32)
    for k in range(groups):
        high, low = split(full[k])
        parts[k, pl.ds(0, nb), :] = high
        parts[k, pl.ds(nb, nb), :] = low
        product = product + dot_nt(high, parts[k])
    cross = product[:, nb:]
    raw_src[...] = product[:, :nb] + cross + cross.T
    raw_copies = [band_copy(raw_src, raw_in, raw_send, raw_recv, r) for r in shifts]
    for copy in raw_copies:
        copy.start()
    raw_in[band] = raw_src[...]
    for copy in raw_copies:
        copy.wait()
    raw = raw_in[0]
    for b in range(1, n_band):
        raw = raw + raw_in[b]
    norm = jnp.sqrt(jnp.sum(raw * raw, keepdims=True))
    scaling = jnp.sqrt(float(grid**3) / norm)
    gram = raw / norm
    linear = 1.5 * eye - 0.5 * gram
    cubic = dot(dot(linear, gram, HIGHEST), dot(linear, linear, HIGHEST), HIGHEST)
    poly = scaling * (1.5 * linear - 0.5 * cubic)
    poly_high, poly_low = split(poly)
    poly_twice = jnp.concatenate([poly_high, poly_high], 1)
    for j in range(groups):
        rotated = dot(poly_twice, parts[j]) + dot(poly_low, parts[j, pl.ds(0, nb), :])
        result[j] = rotated
        row = jnp.sum(occupation * (rotated * rotated), axis=0, keepdims=True) * (1.0 / nb)
        for i in range(pack):
            fresh_src[pl.ds(j * pack + i, 1), :] = row[:, i * cells : (i + 1) * cells]

    fresh_copies = [dom_copy(fresh_src, fresh_all, fr_send, fr_recv, r) for r in range(1, n_dom)]
    for copy in fresh_copies:
        copy.start()
    fresh_all[dom] = fresh_src[...]
    for j in range(groups):
        out_ref[j] = result[j].T
    for copy in din_copies:
        copy.wait()

    def ordered(ref):
        rows = []
        for p in range(n_dom):
            total = jnp.zeros((ROWS, cells), F32)
            for d in range(n_dom):
                total = total + jnp.where(places[d] == p, 1.0, 0.0).astype(F32) * ref[d]
            rows.append(total)
        return rows

    inflow = ordered(din_all)
    for copy in fresh_copies:
        copy.wait()
    fresh = ordered(fresh_all)

    gap = grid - BUFFER
    mix_new = jnp.full((1, cells), mix_ref[0].astype(F32))
    mix_old = jnp.full((1, cells), mix_ref[1].astype(F32))
    mixed = []
    own_density = jnp.zeros((ROWS, cells), F32)
    for p in range(n_dom):
        own = fresh[p]
        blended = own
        if p > 0:
            left = jnp.concatenate([fresh[p - 1][:, gap:], fresh[p - 1][:, :gap]], 1)
            low = (weight * left + (BLEND_TOTAL - weight) * own) / BLEND_TOTAL
            blended = jnp.where(z < BUFFER, low, blended)
        if p < n_dom - 1:
            right = jnp.concatenate([fresh[p + 1][:, cells - gap :], fresh[p + 1][:, : cells - gap]], 1)
            high = (weight * own + (BLEND_TOTAL - weight) * right) / BLEND_TOTAL
            blended = jnp.where(z >= gap, high, blended)
        value = (mix_new * blended + mix_old * inflow[p]) / (mix_new + mix_old)
        mixed.append(value)
        own_density = own_density + jnp.where(own_place == p, 1.0, 0.0).astype(F32) * value
    den_ref[:, 0, :] = own_density[:planes]

    stacked = jnp.concatenate(mixed, 0)
    height = n_dom * ROWS
    high, low = split(stacked)
    both = dot(jnp.concatenate([high, low], 0), coarsen_ref[...])
    coarse = both[:height] + both[height:]
    wide = jnp.concatenate([coarse[p * ROWS : (p + 1) * ROWS] for p in range(n_dom)], 1)
    high, low = split(wide)
    spec_src[...] = dot(high, sph_ref[...]) + dot(low, sph_ref[...]) + dot(high, spl_ref[...])
    spec_copies = [band_copy(spec_src, spec_all, sp_send, sp_recv, r) for r in shifts]
    for copy in spec_copies:
        copy.start()
    spec_all[band] = spec_src[...]
    for copy in spec_copies:
        copy.wait()
    gathered = spec_all[...].reshape(n_band * ROWS, spec_src.shape[1])
    spectrum = dot(fwd_ref[...], gathered, HIGHEST) * inv_ref[...]
    mine = dot(bwd_ref[pl.ds(pl.multiple_of(band * ROWS, ROWS), ROWS), :], spectrum, HIGHEST)
    high, low = split(mine)
    field = dot_nt(high, own_h[...]) + dot_nt(low, own_h[...]) + dot_nt(high, own_l[...])
    for cell in range(CZ):
        har_ref[cell] = field[: har_ref.shape[1], cell * CG : (cell + 1) * CG]


def body(orbitals, potential, density_in, occupation, position, mixing, correlation_weight):
    nb = occupation.shape[0]
    n_dom, n_band = lax.axis_size("dom"), lax.axis_size("band")
    _, local, grid, cells = orbitals.shape
    planes = density_in.shape[1]
    coarse_x = planes // COARSEN
    chain = CG * CZ * n_dom
    pack = 2 if planes % 2 == 0 else 1
    groups = planes // pack
    wide_cells = -(-(cells + grid) // 128) * 128
    sizes = (grid, cells, nb, local, planes, pack, n_dom, n_band)
    vmem = pl.BlockSpec(memory_space=pltpu.VMEM)
    smem = pl.BlockSpec(memory_space=pltpu.SMEM)
    consts = [jnp.asarray(t) for t in tables(grid, n_dom, n_band)]
    dma = pltpu.SemaphoreType.DMA
    chunks = local // 8
    out, density, hartree = pl.pallas_call(
        functools.partial(kernel, sizes),
        out_shape=(
            jax.ShapeDtypeStruct((groups, pack * cells, nb), F32),
            jax.ShapeDtypeStruct((planes, 1, cells), F32),
            jax.ShapeDtypeStruct((CZ, coarse_x, CG), F32),
        ),
        in_specs=[vmem] * 4 + [smem] * 3 + [vmem] * 6,
        out_specs=(vmem, vmem, vmem),
        scratch_shapes=[
            pltpu.VMEM((grid, 8, wide_cells), F32),
            pltpu.VMEM((grid, 8, wide_cells), F32),
            pltpu.VMEM((grid, 8, wide_cells), F32),
            pltpu.VMEM((grid // pack, local, pack * cells), F32),
            pltpu.VMEM((groups, nb, pack * cells), F32),
            pltpu.VMEM((groups, nb, pack * cells), F32),
            pltpu.VMEM((groups, 2 * nb, pack * cells), BF16),
            pltpu.VMEM((nb, nb), F32),
            pltpu.VMEM((n_band, nb, nb), F32),
            pltpu.VMEM((ROWS, cells), F32),
            pltpu.VMEM((n_dom, ROWS, cells), F32),
            pltpu.VMEM((ROWS, cells), F32),
            pltpu.VMEM((n_dom, ROWS, cells), F32),
            pltpu.VMEM((ROWS, chain), F32),
            pltpu.VMEM((n_band, ROWS, chain), F32),
            pltpu.VMEM((CG * CZ, chain), BF16),
            pltpu.VMEM((CG * CZ, chain), BF16),
            dma((n_band - 1, chunks)), dma((n_band - 1, chunks)),
            dma((n_band - 1,)), dma((n_band - 1,)),
            dma((n_dom - 1,)), dma((n_dom - 1,)),
            dma((n_dom - 1,)), dma((n_dom - 1,)),
            dma((n_band - 1,)), dma((n_band - 1,)),
        ],
        compiler_params=pltpu.CompilerParams(
            collective_id=0, has_side_effects=True, vmem_limit_bytes=56 * 1024 * 1024
        ),
    )(
        orbitals[0], potential[0], jnp.swapaxes(density_in, 0, 1), occupation.reshape(1, nb),
        position, mixing, correlation_weight, *consts,
    )
    return (
        jnp.transpose(out.reshape(planes, cells, nb), (2, 0, 1))[None],
        jnp.swapaxes(density, 0, 1),
        jnp.transpose(hartree, (1, 2, 0))[None],
    )


def solution(mesh):
    return jax.shard_map(
        body,
        mesh=mesh,
        in_specs=(
            P("dom", "band", None, None),
            P("dom", None, None),
            P("dom", "band", None),
            P(),
            P(),
            P(),
            P(),
        ),
        out_specs=(
            P("dom", None, "band", None),
            P("dom", "band", None),
            P("dom", "band", None, None),
        ),
        check_vma=False,
    )
```

```python
import functools

import jax
import jax.numpy as jnp
import ml_dtypes
import numpy as np
from jax import lax
from jax.experimental import pallas as pl
from jax.experimental.pallas import tpu as pltpu
from jax.sharding import PartitionSpec as P

BUFFER = 6
COARSEN = 3
CG = 8
CZ = 6
ROWS = 8
CENTER = 5.25
HALF_WIDTH = 4.25
BLEND_TOTAL = 16.0
HIGHEST = lax.Precision.HIGHEST
MESH = pl.DeviceIdType.MESH
F32, BF16 = jnp.float32, jnp.bfloat16


def split_np(table):
    high = table.astype(ml_dtypes.bfloat16)
    return high, (table - high.astype(np.float64)).astype(ml_dtypes.bfloat16)


def tables(grid, dom_count, band_count):
    along_y = np.zeros((grid, CG))
    along_y[np.arange(grid), np.arange(grid) // COARSEN] = 1.0
    along_z = np.zeros((grid, CZ))
    core = np.arange(CZ * COARSEN)
    along_z[core, core // COARSEN] = 1.0
    coarsen = np.einsum("yY,zZ->yzZY", along_y, along_z).reshape(grid * grid, CZ * CG)
    order = np.arange(CG)
    cosine = np.sqrt(2.0 / CG) * np.cos(np.pi * order[:, None] * (order[None, :] + 0.5) / CG)
    cosine[0] *= np.sqrt(0.5)
    chain = dom_count * CZ
    place = np.arange(chain)
    sine = np.sqrt(2.0 / (chain + 1)) * np.sin(
        np.pi * (place[:, None] + 1.0) * (place[None, :] + 1.0) / (chain + 1)
    )
    spectral = np.einsum("ky,pzq->pzykq", cosine, sine.reshape(dom_count, CZ, chain)).reshape(
        dom_count * CG * CZ, CG * chain
    )
    planes = grid // band_count
    coarse_x = planes // COARSEN
    forward = np.zeros((CG, band_count, ROWS))
    backward = np.zeros((band_count, ROWS, CG))
    for band in range(band_count):
        for plane in range(planes):
            forward[:, band, plane] = cosine[:, band * coarse_x + plane // COARSEN] / COARSEN**3
        for cell in range(coarse_x):
            backward[band, cell] = cosine[:, band * coarse_x + cell]
    side = 4.0 * np.sin(0.5 * np.pi * order / CG) ** 2
    depth = 4.0 * np.sin(0.5 * np.pi * (place + 1.0) / (chain + 1.0)) ** 2
    eigen = side[:, None, None] + side[None, :, None] + depth[None, None, :]
    inverse = (8.0 / chain**2 / eigen).reshape(CG, CG * chain)
    spectral_high, spectral_low = split_np(spectral)
    return (
        coarsen.astype(ml_dtypes.bfloat16),
        spectral_high,
        spectral_low,
        forward.reshape(CG, band_count * ROWS).astype(np.float32),
        backward.reshape(band_count * ROWS, CG).astype(np.float32),
        inverse.astype(np.float32),
    )


def split(values):
    high = values.astype(BF16)
    return high, (values - high.astype(F32)).astype(BF16)


def dot(a, b, precision=None):
    return jnp.dot(a, b, preferred_element_type=F32, precision=precision)


def dot_nt(a, b):
    return lax.dot_general(a, b, (((1,), (1,)), ((), ())), preferred_element_type=F32)


def kernel(
    sizes,
    orb_ref, pot_ref, din_ref, occ_ref, pos_ref, mix_ref, cw_ref,
    coarsen_ref, sph_ref, spl_ref, fwd_ref, bwd_ref, inv_ref,
    out_ref, den_ref, har_ref,
    diag, before, once, filt, full, result, parts, raw_src, raw_in, din_src, din_all, fresh_src, fresh_all,
    spec_src, spec_all, own_h, own_l,
    a2a_send, a2a_recv, raw_send, raw_recv, din_send, din_recv, fr_send, fr_recv, sp_send, sp_recv,
):
    grid, cells, nb, local, planes, pack, n_dom, n_band = sizes
    groups = planes // pack
    dom, band = lax.axis_index("dom"), lax.axis_index("band")
    shifts = [r for r in range(1, n_band)]
    shifts.sort(key=lambda r: r % 2)
    chunks = local // 8

    barrier = pltpu.get_barrier_semaphore()
    for r in range(1, n_band):
        pl.semaphore_signal(barrier, inc=1, device_id={"band": lax.rem(band + r, n_band)}, device_id_type=MESH)
    for r in range(1, n_dom):
        pl.semaphore_signal(barrier, inc=1, device_id={"dom": lax.rem(dom + r, n_dom)}, device_id_type=MESH)

    wide_cells = diag.shape[2]
    lane = lax.broadcasted_iota(jnp.int32, (8, wide_cells), 1)
    depth = lax.rem(lane, grid)
    inside = jnp.where(lane < cells, 1.0, 0.0).astype(F32)
    above = jnp.where((lane < cells) & (depth > 0), 1.0, 0.0).astype(F32)
    below = jnp.where((lane < cells) & (depth < grid - 1), 1.0, 0.0).astype(F32)
    for k in range(grid):
        row = (3.0 - CENTER + pot_ref[pl.ds(k, 1), :]) * (1.0 / HALF_WIDTH)
        diag[k, :, pl.ds(0, cells)] = jnp.broadcast_to(row, (8, cells))
        for ref in (diag, before):
            ref[k, :, pl.ds(cells, wide_cells - cells)] = jnp.zeros((8, wide_cells - cells), F32)
    if planes < ROWS:
        din_src[...] = jnp.zeros_like(din_src)
        fresh_src[...] = jnp.zeros_like(fresh_src)
    din_src[pl.ds(0, planes), :] = din_ref[:, 0, :]

    def shifted(ref, k):
        here = ref[k]
        total = pltpu.roll(here, grid, 1) + pltpu.roll(here, wide_cells - grid, 1)
        total = total + above * pltpu.roll(here, 1, 1) + below * pltpu.roll(here, wide_cells - 1, 1)
        if k > 0:
            total = total + ref[k - 1]
        if k < grid - 1:
            total = total + ref[k + 1]
        return diag[k] * here - (0.5 / HALF_WIDTH) * total

    def a2a_copy(r, c, start):
        peer = lax.rem(band + r, n_band)
        return pltpu.make_async_remote_copy(
            src_ref=filt.at[pl.ds(peer * groups, groups), pl.ds(start, 8), :],
            dst_ref=full.at[:, pl.ds(pl.multiple_of(band * local + start, 8), 8), :],
            send_sem=a2a_send.at[r - 1, c],
            recv_sem=a2a_recv.at[r - 1, c],
            device_id={"band": peer},
            device_id_type=MESH,
        )

    def filter_chunk(c):
        start = pl.multiple_of(c * 8, 8)
        before[:, :, pl.ds(0, cells)] = jnp.swapaxes(orb_ref[pl.ds(start, 8)], 0, 1)
        for k in range(grid):
            once[k] = inside * shifted(before, k)
        for j in range(grid // pack):
            pieces = [
                (2.0 * shifted(once, k) - before[k])[:, :cells] for k in range(j * pack, (j + 1) * pack)
            ]
            filt[j, pl.ds(start, 8), :] = pieces[0] if pack == 1 else jnp.concatenate(pieces, 1)

    def send_chunk(c):
        start = pl.multiple_of(c * 8, 8)
        for r in shifts:
            a2a_copy(r, c, start).start()
        full[:, pl.ds(pl.multiple_of(band * local + start, 8), 8), :] = filt[
            pl.ds(band * groups, groups), pl.ds(start, 8), :
        ]

    filter_chunk(0)
    pl.semaphore_wait(barrier, n_band + n_dom - 2)
    send_chunk(0)

    def step(c, carry):
        filter_chunk(c)
        send_chunk(c)
        return carry

    lax.fori_loop(1, chunks, step, 0)

    def dom_copy(src, dst, send, recv, r):
        return pltpu.make_async_remote_copy(
            src_ref=src, dst_ref=dst.at[dom], send_sem=send.at[r - 1], recv_sem=recv.at[r - 1],
            device_id={"dom": lax.rem(dom + r, n_dom)}, device_id_type=MESH,
        )

    def band_copy(src, dst, send, recv, r):
        return pltpu.make_async_remote_copy(
            src_ref=src, dst_ref=dst.at[band], send_sem=send.at[r - 1], recv_sem=recv.at[r - 1],
            device_id={"band": lax.rem(band + r, n_band)}, device_id_type=MESH,
        )

    din_copies = [dom_copy(din_src, din_all, din_send, din_recv, r) for r in range(1, n_dom)]
    for copy in din_copies:
        copy.start()
    din_all[dom] = din_src[...]

    places = [pos_ref[d] for d in range(n_dom)]
    own_place = jnp.int32(0)
    for d in range(n_dom):
        own_place = own_place + jnp.where(dom == d, places[d], 0)
    block = CG * CZ
    total_h = jnp.zeros(own_h.shape, F32)
    total_l = jnp.zeros(own_l.shape, F32)
    for p in range(n_dom):
        pick = jnp.where(own_place == p, 1.0, 0.0).astype(F32)
        total_h = total_h + pick * sph_ref[pl.ds(p * block, block), :].astype(F32)
        total_l = total_l + pick * spl_ref[pl.ds(p * block, block), :].astype(F32)
    own_h[...] = total_h.astype(BF16)
    own_l[...] = total_l.astype(BF16)
    z = lax.rem(lax.broadcasted_iota(jnp.int32, (1, cells), 1), grid)
    weight = jnp.zeros((1, cells), F32)
    for j in range(BUFFER):
        value = cw_ref[j].astype(F32)
        weight = weight + jnp.where((z == j) | (z == grid - BUFFER + j), value, 0.0)
    row_id = lax.broadcasted_iota(jnp.int32, (nb, nb), 0)
    col_id = lax.broadcasted_iota(jnp.int32, (nb, nb), 1)
    eye = jnp.where(row_id == col_id, 1.0, 0.0).astype(F32)
    occupation = jnp.sum(eye * occ_ref[...], axis=1, keepdims=True)

    def wait_chunk(c, carry):
        start = pl.multiple_of(c * 8, 8)
        for r in shifts:
            a2a_copy(r, c, start).wait()
        return carry

    lax.fori_loop(0, chunks, wait_chunk, 0)

    product = jnp.zeros((nb, 2 * nb), F32)
    for k in range(groups):
        high, low = split(full[k])
        parts[k, pl.ds(0, nb), :] = high
        parts[k, pl.ds(nb, nb), :] = low
        product = product + dot_nt(high, parts[k])
    cross = product[:, nb:]
    raw_src[...] = product[:, :nb] + cross + cross.T
    raw_copies = [band_copy(raw_src, raw_in, raw_send, raw_recv, r) for r in shifts]
    for copy in raw_copies:
        copy.start()
    raw_in[band] = raw_src[...]
    for copy in raw_copies:
        copy.wait()
    raw = raw_in[0]
    for b in range(1, n_band):
        raw = raw + raw_in[b]
    norm = jnp.sqrt(jnp.sum(raw * raw, keepdims=True))
    scaling = jnp.sqrt(float(grid**3) / norm)
    gram = raw / norm
    linear = 1.5 * eye - 0.5 * gram
    cubic = dot(dot(linear, gram, HIGHEST), dot(linear, linear, HIGHEST), HIGHEST)
    poly = scaling * (1.5 * linear - 0.5 * cubic)
    poly_high, poly_low = split(poly)
    poly_twice = jnp.concatenate([poly_high, poly_high], 1)
    for j in range(groups):
        rotated = dot(poly_twice, parts[j]) + dot(poly_low, parts[j, pl.ds(0, nb), :])
        result[j] = rotated
        row = jnp.sum(occupation * (rotated * rotated), axis=0, keepdims=True) * (1.0 / nb)
        for i in range(pack):
            fresh_src[pl.ds(j * pack + i, 1), :] = row[:, i * cells : (i + 1) * cells]

    fresh_copies = [dom_copy(fresh_src, fresh_all, fr_send, fr_recv, r) for r in range(1, n_dom)]
    for copy in fresh_copies:
        copy.start()
    fresh_all[dom] = fresh_src[...]
    for j in range(groups):
        out_ref[j] = result[j].T
    for copy in din_copies:
        copy.wait()

    def ordered(ref):
        rows = []
        for p in range(n_dom):
            total = jnp.zeros((ROWS, cells), F32)
            for d in range(n_dom):
                total = total + jnp.where(places[d] == p, 1.0, 0.0).astype(F32) * ref[d]
            rows.append(total)
        return rows

    inflow = ordered(din_all)
    for copy in fresh_copies:
        copy.wait()
    fresh = ordered(fresh_all)

    gap = grid - BUFFER
    mix_new = jnp.full((1, cells), mix_ref[0].astype(F32))
    mix_old = jnp.full((1, cells), mix_ref[1].astype(F32))
    mixed = []
    own_density = jnp.zeros((ROWS, cells), F32)
    for p in range(n_dom):
        own = fresh[p]
        blended = own
        if p > 0:
            left = jnp.concatenate([fresh[p - 1][:, gap:], fresh[p - 1][:, :gap]], 1)
            low = (weight * left + (BLEND_TOTAL - weight) * own) / BLEND_TOTAL
            blended = jnp.where(z < BUFFER, low, blended)
        if p < n_dom - 1:
            right = jnp.concatenate([fresh[p + 1][:, cells - gap :], fresh[p + 1][:, : cells - gap]], 1)
            high = (weight * own + (BLEND_TOTAL - weight) * right) / BLEND_TOTAL
            blended = jnp.where(z >= gap, high, blended)
        value = (mix_new * blended + mix_old * inflow[p]) / (mix_new + mix_old)
        mixed.append(value)
        own_density = own_density + jnp.where(own_place == p, 1.0, 0.0).astype(F32) * value
    den_ref[:, 0, :] = own_density[:planes]

    stacked = jnp.concatenate(mixed, 0)
    height = n_dom * ROWS
    high, low = split(stacked)
    both = dot(jnp.concatenate([high, low], 0), coarsen_ref[...])
    coarse = both[:height] + both[height:]
    wide = jnp.concatenate([coarse[p * ROWS : (p + 1) * ROWS] for p in range(n_dom)], 1)
    high, low = split(wide)
    spec_src[...] = dot(high, sph_ref[...]) + dot(low, sph_ref[...]) + dot(high, spl_ref[...])
    spec_copies = [band_copy(spec_src, spec_all, sp_send, sp_recv, r) for r in shifts]
    for copy in spec_copies:
        copy.start()
    spec_all[band] = spec_src[...]
    for copy in spec_copies:
        copy.wait()
    gathered = spec_all[...].reshape(n_band * ROWS, spec_src.shape[1])
    spectrum = dot(fwd_ref[...], gathered, HIGHEST) * inv_ref[...]
    mine = dot(bwd_ref[pl.ds(pl.multiple_of(band * ROWS, ROWS), ROWS), :], spectrum, HIGHEST)
    high, low = split(mine)
    field = dot_nt(high, own_h[...]) + dot_nt(low, own_h[...]) + dot_nt(high, own_l[...])
    for cell in range(CZ):
        har_ref[cell] = field[: har_ref.shape[1], cell * CG : (cell + 1) * CG]


def hand_over(out_ref, den_ref, har_ref, out_last, den_last, har_last, sems):
    pieces = out_ref.shape[0]
    copies = [pltpu.make_async_copy(out_ref.at[k], out_last.at[k], sems.at[k]) for k in range(pieces)]
    for copy in copies:
        copy.start()
    den_last[...] = den_ref[...]
    har_last[...] = har_ref[...]
    for copy in copies:
        copy.wait()


def body(orbitals, potential, density_in, occupation, position, mixing, correlation_weight):
    nb = occupation.shape[0]
    n_dom, n_band = lax.axis_size("dom"), lax.axis_size("band")
    _, local, grid, cells = orbitals.shape
    planes = density_in.shape[1]
    coarse_x = planes // COARSEN
    chain = CG * CZ * n_dom
    pack = 2 if planes % 2 == 0 else 1
    groups = planes // pack
    wide_cells = -(-(cells + grid) // 128) * 128
    sizes = (grid, cells, nb, local, planes, pack, n_dom, n_band)
    vmem = pl.BlockSpec(memory_space=pltpu.VMEM)
    smem = pl.BlockSpec(memory_space=pltpu.SMEM)
    consts = [jnp.asarray(t) for t in tables(grid, n_dom, n_band)]
    dma = pltpu.SemaphoreType.DMA
    chunks = local // 8
    out, density, hartree = pl.pallas_call(
        functools.partial(kernel, sizes),
        out_shape=(
            jax.ShapeDtypeStruct((groups, pack * cells, nb), F32),
            jax.ShapeDtypeStruct((planes, 1, cells), F32),
            jax.ShapeDtypeStruct((CZ, coarse_x, CG), F32),
        ),
        in_specs=[vmem] * 4 + [smem] * 3 + [vmem] * 6,
        out_specs=(vmem, vmem, vmem),
        scratch_shapes=[
            pltpu.VMEM((grid, 8, wide_cells), F32),
            pltpu.VMEM((grid, 8, wide_cells), F32),
            pltpu.VMEM((grid, 8, wide_cells), F32),
            pltpu.VMEM((grid // pack, local, pack * cells), F32),
            pltpu.VMEM((groups, nb, pack * cells), F32),
            pltpu.VMEM((groups, nb, pack * cells), F32),
            pltpu.VMEM((groups, 2 * nb, pack * cells), BF16),
            pltpu.VMEM((nb, nb), F32),
            pltpu.VMEM((n_band, nb, nb), F32),
            pltpu.VMEM((ROWS, cells), F32),
            pltpu.VMEM((n_dom, ROWS, cells), F32),
            pltpu.VMEM((ROWS, cells), F32),
            pltpu.VMEM((n_dom, ROWS, cells), F32),
            pltpu.VMEM((ROWS, chain), F32),
            pltpu.VMEM((n_band, ROWS, chain), F32),
            pltpu.VMEM((CG * CZ, chain), BF16),
            pltpu.VMEM((CG * CZ, chain), BF16),
            dma((n_band - 1, chunks)), dma((n_band - 1, chunks)),
            dma((n_band - 1,)), dma((n_band - 1,)),
            dma((n_dom - 1,)), dma((n_dom - 1,)),
            dma((n_dom - 1,)), dma((n_dom - 1,)),
            dma((n_band - 1,)), dma((n_band - 1,)),
        ],
        compiler_params=pltpu.CompilerParams(
            collective_id=0, has_side_effects=True, vmem_limit_bytes=56 * 1024 * 1024
        ),
    )(
        orbitals[0], potential[0], jnp.swapaxes(density_in, 0, 1), occupation.reshape(1, nb),
        position, mixing, correlation_weight, *consts,
    )
    any_space = pl.BlockSpec(memory_space=pl.ANY)
    out = out.reshape(planes, cells, nb)
    out, density, hartree = pl.pallas_call(
        hand_over,
        out_shape=tuple(jax.ShapeDtypeStruct(a.shape, F32) for a in (out, density, hartree)),
        in_specs=[any_space, vmem, vmem],
        out_specs=(any_space, vmem, vmem),
        scratch_shapes=[dma((planes,))],
    )(out, density, hartree)
    return (
        jnp.transpose(out, (2, 0, 1))[None],
        jnp.swapaxes(density, 0, 1),
        jnp.transpose(hartree, (1, 2, 0))[None],
    )


def solution(mesh):
    return jax.shard_map(
        body,
        mesh=mesh,
        in_specs=(
            P("dom", "band", None, None),
            P("dom", None, None),
            P("dom", "band", None),
            P(),
            P(),
            P(),
            P(),
        ),
        out_specs=(
            P("dom", None, "band", None),
            P("dom", "band", None),
            P("dom", "band", None, None),
        ),
        check_vma=False,
    )
```
